32 devices in a mesh: tile: 4 (over z), orbit: 8 (over y, x, core).
Axes of the slice: x: 2, y: 2, z: 4, core: 2. Of those that a mesh axis runs over, the one named last changes fastest.
Arguments:
- jacobians: bfloat16 [4096, 128, 3, 128], P(('tile', 'orbit')), may hold values from -1.5 to 1.5
- point_normals: float32 [4096, 6, 128], P(('tile', 'orbit')), as said below
- block_counts: int32 [32, 128], P(('tile', 'orbit')), may hold values from 1 to 128, 8192 in all within a row
- pair_owner: int32 [4096, 1], P(('tile', 'orbit')), may hold values from 0 to 7; in each aligned block of 128 rows (0 to 127, 128 to 255, ...) at most 32 rows name the same one
- pair_local: int32 [4096], P(('tile', 'orbit')), may hold values from 0 to 255
- crossing: int32 [8], replicated, may hold values from 0 to 7, as said below
Outputs:
- coupled: float32 [8, 256, 4096], P('orbit', 'tile')
The draws below stay inside these ranges and needn't reach their ends.
Inputs may be any that keep to these rules, and one draw needn't show every extreme that they name: `point_normals`: each 3x3 block is symmetric, and in every row the diagonal entry exceeds the sum of the off-diagonal magnitudes by 0.2 or more. `pair_owner`: among the 128 rows of one device no owner appears more than 32 times. crossing[crossing[o]] = o and crossing[o] != o for every orbit o.
All inputs are finite; a program needn't handle non-finite values.
Results may differ from the reference program's by a relative error of at most 0.0029.
Values sent between devices are 32-bit elements; how exact they have to be, the bound alone decides.
A program may use at most 128 MiB of HBM per device.

```python
import math
import jax
import jax.numpy as jnp
import numpy as np
from jax import lax

P_SIZE = 64
PTS = 128
SLOT_DEV = 128
PAIR_ORB = 256
ORBITS = 8
GROUPS = 32
SLOTS_ALL = 4096
NPAIR = 2048
CAP = 32


def draw_point_normals(key, part):
    key_diag, key_off = jax.random.split(key)
    diagonal = 1.2 + 0.6 * jax.random.uniform(key_diag, (SLOTS_ALL, 3, PTS), jnp.float32)
    off_part = jax.random.uniform(key_off, (SLOTS_ALL, 3, PTS), jnp.float32, -0.5, 0.5)
    return jnp.concatenate([diagonal, off_part], axis=1).astype(jnp.float32)


def draw_crossing(key, part):
    order = jax.random.permutation(key, ORBITS).astype(jnp.int32)
    partner_pos = jnp.arange(ORBITS, dtype=jnp.int32) ^ 1
    return jnp.zeros((ORBITS,), jnp.int32).at[order].set(order[partner_pos])


def with_ends(values, stream_key, smallest, largest):
    longest = values.shape.index(max(values.shape))
    spots = []
    for shift in (0, 1):
        where = [jax.random.randint(jax.random.fold_in(stream_key, axis), (), 0, length) for axis, length in enumerate(values.shape)]
        where[longest] = (where[longest] + shift) % values.shape[longest]
        spots.append(tuple(where))
    return values.at[spots[0]].set(smallest).at[spots[1]].set(largest)


def shard_levels(own_key, shape, shards, low, largest):
    gain = 1.0
    for position, blocks in shards:
        heights = jax.random.uniform(jax.random.fold_in(jax.random.fold_in(own_key, 6), position), (blocks,), jnp.float32, low / len(shards), largest / len(shards))
        gain = gain * jnp.repeat(jnp.exp(heights), shape[position] // blocks).reshape((-1,) + (1,) * (len(shape) - 1 - position))
    return gain


def split_up(number_of, total, most, lean):
    weights = [(1 << 20) // math.isqrt(rank ** lean) + 1 for rank in range(2, number_of + 1)]
    rest, given = total - most - (number_of - 1), [1] * (number_of - 1)
    while rest > 0:
        candidates = [i for i in range(number_of - 1) if given[i] < most]
        whole, budget = sum([weights[i] for i in candidates]), rest
        for i in candidates:
            more = min(most - given[i], max(1, budget * weights[i] // whole), rest)
            given[i] = given[i] + more
            rest = rest - more
    return np.array([most] + given)


def ragged_sizes(own_key, number_of, total, most, skew):
    if number_of == 2:
        one = jax.random.randint(own_key, (), max(1, total - most), min(most, total - 1) + 1)
        return jnp.stack([one, total - one])
    tallies = jnp.asarray(split_up(number_of, total, most, skew), jnp.int32)
    pairs = (number_of - 1) // 2
    source_of, receiver = tallies[1:1 + 2 * pairs:2], tallies[2:2 + 2 * pairs:2]
    slack = jnp.minimum(source_of - 1, most - receiver)
    passed = jax.random.randint(jax.random.fold_in(own_key, 1), (pairs,), 0, 1 << 20) % (slack + 1)
    tallies = tallies.at[1:1 + 2 * pairs:2].set(source_of - passed).at[2:2 + 2 * pairs:2].set(receiver + passed)
    return tallies[jax.random.permutation(jax.random.fold_in(own_key, 2), number_of)]


def assign_block(rng, own, number, rows, number_of, top, reach, lean):
    order = jax.random.permutation(rng, number_of)
    packed, common = load_shares(number_of, rows * top, reach, lean, True), load_shares(number_of, rows * top, reach, lean, False)
    places = jnp.arange(number_of)

    def named(lengths, offset_by):
        used = int((lengths > 0).sum())
        fixed = max(1, used // 4)
        passed = fixed + (places - fixed + offset_by * (used - fixed)) % max(1, number_of - fixed)
        return jnp.zeros((number_of,), jnp.int32).at[order[jnp.where(places < fixed, places, passed)]].set(jnp.asarray(lengths, jnp.int32))

    lengths = jnp.where(number % 4 == 0, named(packed, number // 4), named(common, number - number // 4 - 1))
    mixed = jax.random.permutation(jax.random.fold_in(own, 3), number_of)
    donor, sink = mixed[0:number_of // 2 * 2:2], mixed[1:number_of // 2 * 2:2]
    margin = jnp.minimum(lengths[donor] - 1, reach - lengths[sink]) // 2
    margin = jnp.where((donor == order[0]) | (sink == order[0]) | (lengths[sink] == 0), 0, jnp.maximum(margin, 0))
    passed = jax.random.randint(jax.random.fold_in(own, 4), (number_of // 2,), 0, 1 << 20) % (margin + 1)
    lengths = lengths.at[donor].add(-passed).at[sink].add(passed)
    items = jnp.searchsorted(jnp.cumsum(lengths), jnp.arange(rows * top), side="right").astype(jnp.int32)
    grid = items.reshape(top, rows).T
    grid = grid[jax.random.permutation(jax.random.fold_in(own, 1), rows)]
    offset_by = jax.random.randint(jax.random.fold_in(own, 2), (rows, 1), 0, top)
    return jnp.take_along_axis(grid, (jnp.arange(top)[None, :] + offset_by) % top, axis=1)


def load_shares(count, total, bound, slope, full):
    portions = [(1 << 20) // math.isqrt(rank ** slope) + 1 for rank in range(1, count + 1)]
    largest = bound if full else min(bound, max(-(-total // count), total * portions[0] // sum(portions)))
    least = 1 if total - largest >= count - 1 else 0
    given, spare = [largest] + [least] * (count - 1), total - largest - least * (count - 1)
    while spare > 0:
        movable = [i for i in range(1, count) if given[i] < largest] or [i for i in range(1, count) if given[i] < bound]
        mass, left = sum([portions[i] for i in movable]), spare
        for i in movable:
            extra = min(bound - given[i], max(1, left * portions[i] // mass), spare)
            given[i] = given[i] + extra
            spare = spare - extra
    return np.array(given)


def scatter_about(key, shape, scale, reach, shards=(), held_as=jnp.bfloat16):
    values = jax.random.normal(key, shape, jnp.float32) * scale
    if len(shards) > 0:
        values = shard_levels(key, shape, shards, -0.22, 0.18) * values
    return jnp.clip(values, min=-reach, max=reach).astype(held_as)


def setup_inputs(seed: int = 0) -> dict:
    streams_of = jax.random.split(jax.random.key(seed), 7)
    jacobians = scatter_about(streams_of[0], (SLOTS_ALL, PTS, 3, 2 * P_SIZE), 0.25, 1.5, ((0, 32),))
    point_normals = draw_point_normals(jax.random.fold_in(streams_of[6], 71), 0)
    block_counts = jax.vmap(lambda own: ragged_sizes(own, SLOT_DEV, SLOT_DEV * PTS // 2, PTS, 2))(jax.random.split(streams_of[2], GROUPS)).reshape((GROUPS, SLOT_DEV)).astype(jnp.int32)
    pair_owner_keys = jax.random.split(jax.random.fold_in(streams_of[3], 1), SLOTS_ALL // SLOT_DEV)
    pair_owner_turns = jax.random.permutation(jax.random.fold_in(streams_of[3], 3), SLOTS_ALL // SLOT_DEV)
    pair_owner = jax.vmap(lambda own, number: assign_block(jax.random.fold_in(streams_of[3], 2), own, number, SLOT_DEV, ORBITS, 1, CAP, 2))(pair_owner_keys, pair_owner_turns).reshape((SLOTS_ALL, 1))
    pair_local = with_ends(jax.random.randint(streams_of[4], (SLOTS_ALL,), 0, PAIR_ORB), jax.random.fold_in(streams_of[4], 1), 0, PAIR_ORB - 1).astype(jnp.int32)
    crossing = draw_crossing(jax.random.fold_in(streams_of[6], 71), 0)
    return dict(jacobians=jacobians, point_normals=point_normals, block_counts=block_counts, pair_owner=pair_owner, pair_local=pair_local, crossing=crossing)


def eliminate(jacobians, point_normals, counts):
    jac_float = jacobians.astype(jnp.float32)
    left_half = jac_float[..., :P_SIZE]
    right_half = jac_float[..., P_SIZE:]
    diag_one = point_normals[:, 0, :][:, :, None]
    diag_two = point_normals[:, 1, :][:, :, None]
    diag_three = point_normals[:, 2, :][:, :, None]
    off_ab = point_normals[:, 3, :][:, :, None]
    off_ac = point_normals[:, 4, :][:, :, None]
    off_bc = point_normals[:, 5, :][:, :, None]
    cof_aa = diag_two * diag_three - off_bc * off_bc
    cof_bb = diag_one * diag_three - off_ac * off_ac
    cof_cc = diag_one * diag_two - off_ab * off_ab
    cof_ab = off_ac * off_bc - off_ab * diag_three
    cof_ac = off_ab * off_bc - off_ac * diag_two
    cof_bc = off_ab * off_ac - diag_one * off_bc
    determinant = diag_one * cof_aa + off_ab * cof_ab + off_ac * cof_ac
    live_mask = (jnp.arange(PTS, dtype=jnp.int32)[None, :] < counts[:, None]).astype(jnp.float32)
    weight = live_mask[:, :, None] / determinant
    comp_a = right_half[:, :, 0, :]
    comp_b = right_half[:, :, 1, :]
    comp_c = right_half[:, :, 2, :]
    solved = jnp.stack([
        (cof_aa * comp_a + cof_ab * comp_b + cof_ac * comp_c) * weight,
        (cof_ab * comp_a + cof_bb * comp_b + cof_bc * comp_c) * weight,
        (cof_ac * comp_a + cof_bc * comp_b + cof_cc * comp_c) * weight], axis=2)
    solved = lax.optimization_barrier(solved.astype(jnp.bfloat16))
    blocks = jnp.einsum("spci,spcj->sij", left_half, solved.astype(jnp.float32))
    return blocks.reshape(blocks.shape[0], P_SIZE * P_SIZE)


def one_device(pieces):
    return eliminate(pieces[0], pieces[1], pieces[2])


def reference(jacobians, point_normals, block_counts, pair_owner, pair_local, crossing):
    device_jac = jacobians.reshape(GROUPS, SLOT_DEV, PTS, 3, 2 * P_SIZE)
    device_normals = point_normals.reshape(GROUPS, SLOT_DEV, 6, PTS)
    blocks = lax.map(one_device, (device_jac, device_normals, block_counts))
    blocks = blocks.reshape(SLOTS_ALL, P_SIZE * P_SIZE)
    pair_ids = (pair_owner[:, 0] * PAIR_ORB + pair_local).astype(jnp.int32)
    reduced = jax.ops.segment_sum(blocks, pair_ids, num_segments=NPAIR)
    reduced = reduced.reshape(ORBITS, PAIR_ORB, P_SIZE, P_SIZE)
    mirror = jnp.swapaxes(reduced[crossing], 2, 3)
    return (reduced + mirror).reshape(ORBITS, PAIR_ORB, P_SIZE * P_SIZE)
```

```python
import functools

import jax
import jax.numpy as jnp
from jax import lax
from jax.experimental import pallas as pl
from jax.experimental.pallas import tpu as pltpu
from jax.sharding import PartitionSpec as P

PAIR_ORB = 256
LANES = 128


def weights(normals, counts):
    d1, d2, d3, ab, ac, bc = (normals[i] for i in range(6))
    cof_aa = d2 * d3 - bc * bc
    cof_bb = d1 * d3 - ac * ac
    cof_cc = d1 * d2 - ab * ab
    cof_ab = ac * bc - ab * d3
    cof_ac = ab * bc - ac * d2
    cof_bc = ab * ac - d1 * bc
    det = d1 * cof_aa + ab * cof_ab + ac * cof_ac
    places = lax.broadcasted_iota(jnp.int32, det.shape, 1)
    scale = jnp.where(places < counts, 1.0, 0.0) / det
    rows = ((cof_aa, cof_ab, cof_ac), (cof_ab, cof_bb, cof_bc), (cof_ac, cof_bc, cof_cc))
    return [[entry * scale for entry in row] for row in rows]


def slot_block(jac, coef, s, flip):
    params = jac.shape[-1] // 2
    points = jac.shape[-2]
    right = [jnp.transpose(jac[e])[params:].astype(jnp.float32) for e in range(3)]
    solved = [
        (coef[c][0][s : s + 1] * right[0] + coef[c][1][s : s + 1] * right[1] + coef[c][2][s : s + 1] * right[2]).astype(jnp.bfloat16)
        for c in range(3)
    ]
    mirrored = jnp.dot(
        jnp.concatenate(solved, axis=1), jac.reshape(3 * points, 2 * params), preferred_element_type=jnp.float32
    )
    straight = jnp.transpose(mirrored)[:params]
    return jnp.where(flip > 0, mirrored[:, :params], straight)


def blocks_kernel(jac_ref, normals_ref, counts_ref, flip_ref, out_ref, scratch):
    slots, params = jac_ref.shape[0], jac_ref.shape[3] // 2
    chunks, _, width = out_ref.shape
    coef = weights(normals_ref[...], counts_ref[...])
    for s in range(slots):
        scratch[s * params : (s + 1) * params, :] = slot_block(jac_ref[s], coef, s, flip_ref[s : s + 1, :params])
    for tile in range(chunks * width // LANES):
        pieces = [scratch[pl.ds(2 * tile + half, slots, stride=params), :] for half in range(2)]
        c, at = divmod(tile * LANES, width)
        out_ref[c, :, at : at + LANES] = jnp.concatenate(pieces, axis=1)


def oriented_blocks(jac, normals, counts, flip, chunks):
    slots, _, points, both = jac.shape
    params = both // 2
    width = params * params // chunks
    step = min(16, slots)
    return pl.pallas_call(
        blocks_kernel,
        grid=(slots // step,),
        in_specs=[
            pl.BlockSpec((step, 3, points, both), lambda g: (g, 0, 0, 0)),
            pl.BlockSpec((6, step, points), lambda g: (0, g, 0)),
            pl.BlockSpec((step, points), lambda g: (g, 0)),
            pl.BlockSpec((step, points), lambda g: (g, 0)),
        ],
        out_specs=pl.BlockSpec((chunks, step, width), lambda g: (0, g, 0)),
        out_shape=jax.ShapeDtypeStruct((chunks, slots, width), jnp.float32),
        scratch_shapes=[pltpu.VMEM((step * params, params), jnp.float32)],
        compiler_params=pltpu.CompilerParams(vmem_limit_bytes=32 * 1024 * 1024),
    )(jac, normals, counts, flip)


def local(jacobians, point_normals, block_counts, pair_owner, pair_local, crossing):
    slots, points, _, both = jacobians.shape
    params = both // 2
    orbits, tiles = lax.axis_size("orbit"), lax.axis_size("tile")
    couples, share = orbits // 2, PAIR_ORB // tiles
    jac = jnp.transpose(jacobians, (0, 2, 1, 3))
    normals = jnp.transpose(point_normals, (1, 0, 2))
    counts = jnp.broadcast_to(block_counts[0][:, None], (slots, points))
    orbit_ids = jnp.arange(orbits, dtype=jnp.int32)
    leads = orbit_ids < crossing
    couple = jnp.sum((orbit_ids[None, :] < jnp.minimum(orbit_ids, crossing)[:, None]) & leads[None, :], axis=1).astype(jnp.int32)
    owner_hot = pair_owner == orbit_ids[None, :]
    slot_couple = jnp.sum(jnp.where(owner_hot, couple[None, :], 0), axis=1)
    flip = jnp.sum(jnp.where(owner_hot & ~leads[None, :], 1, 0), axis=1)
    flip = jnp.broadcast_to(flip[:, None], (slots, points))
    row = (pair_local // share) * (couples * share) + slot_couple * share + pair_local % share

    blocks = oriented_blocks(jac, normals, counts, flip, orbits)
    arrived = lax.all_to_all(blocks, "orbit", split_axis=0, concat_axis=0, tiled=True).reshape(orbits * slots, -1)
    rows = lax.all_gather(row, "orbit", tiled=True)
    hot = (jnp.arange(couples * PAIR_ORB, dtype=jnp.int32)[:, None] == rows[None, :]).astype(jnp.bfloat16)
    high = lax.reduce_precision(arrived, 8, 7)
    low = arrived - high
    dense = jnp.dot(hot, high.astype(jnp.bfloat16), preferred_element_type=jnp.float32) + jnp.dot(
        hot, low.astype(jnp.bfloat16), preferred_element_type=jnp.float32
    )
    owned = lax.psum_scatter(dense, "tile", scatter_dimension=0, tiled=True)
    owned = owned.reshape(couples, share, -1)[couple]
    parts = lax.all_to_all(owned, "orbit", split_axis=0, concat_axis=0, tiled=True)
    whole = jnp.transpose(parts, (1, 0, 2)).reshape(share, params, params)
    mine = leads[lax.axis_index("orbit")]
    whole = jnp.where(mine, whole, jnp.swapaxes(whole, 1, 2))
    return whole.reshape(1, share, params * params)


def solution(mesh):
    in_specs = (
        P(("tile", "orbit"), None, None, None),
        P(("tile", "orbit"), None, None),
        P(("tile", "orbit"), None),
        P(("tile", "orbit"), None),
        P(("tile", "orbit")),
        P(),
    )
    out_specs = P("orbit", "tile", None)
    return jax.shard_map(local, mesh=mesh, in_specs=in_specs, out_specs=out_specs, check_vma=False)
```

```python
import jax
import jax.numpy as jnp
from jax import lax
from jax.experimental import pallas as pl
from jax.experimental.pallas import tpu as pltpu
from jax.sharding import PartitionSpec as P

PAIR_ORB = 256
LANES = 128
MESH = pl.DeviceIdType.MESH


def weights(normals, counts):
    d1, d2, d3, ab, ac, bc = (normals[i] for i in range(6))
    cof_aa = d2 * d3 - bc * bc
    cof_bb = d1 * d3 - ac * ac
    cof_cc = d1 * d2 - ab * ab
    cof_ab = ac * bc - ab * d3
    cof_ac = ab * bc - ac * d2
    cof_bc = ab * ac - d1 * bc
    det = d1 * cof_aa + ab * cof_ab + ac * cof_ac
    places = lax.broadcasted_iota(jnp.int32, det.shape, 1)
    scale = jnp.where(places < counts, 1.0, 0.0) / det
    rows = ((cof_aa, cof_ab, cof_ac), (cof_ab, cof_bb, cof_bc), (cof_ac, cof_bc, cof_cc))
    return [[entry * scale for entry in row] for row in rows]


def slot_block(jac, coef, s, flip):
    params = jac.shape[-1] // 2
    points = jac.shape[-2]
    right = [jnp.transpose(jac[e])[params:].astype(jnp.float32) for e in range(3)]
    solved = [
        (coef[c][0][s : s + 1] * right[0] + coef[c][1][s : s + 1] * right[1] + coef[c][2][s : s + 1] * right[2]).astype(jnp.bfloat16)
        for c in range(3)
    ]
    mirrored = jnp.dot(
        jnp.concatenate(solved, axis=1), jac.reshape(3 * points, 2 * params), preferred_element_type=jnp.float32
    )
    straight = jnp.transpose(mirrored)[:params]
    return jnp.where(flip > 0, mirrored[:, :params], straight)


def each(low, high, body):
    def step(i, carry):
        body(i)
        return carry

    lax.fori_loop(low, high, step, 0)


def reduce_kernel(
    jac_hbm, normals_ref, counts_ref, flip_ref, ids_ref, couple_ref, fin_ref,
    jac_v, send, arrived, ids_all, hot, halves, dense, passing, stage, scratch,
    jac_sem, ids_ssem, ids_rsem, a_ssem, a_rsem, b_ssem, b_rsem, c_ssem, c_rsem, own_sem,
):
    groups, orbits, tiles = jac_sem.shape[0], arrived.shape[0], dense.shape[0]
    units, share, rank = fin_ref.shape[1], fin_ref.shape[2], dense.shape[2]
    slots, params = jac_v.shape[0], jac_v.shape[3] // 2
    step, half_rows = slots // groups, params // 2
    t, o = lax.axis_index("tile"), lax.axis_index("orbit")

    def peer_of(k):
        return lax.rem(o + k, orbits)

    def jac_copy(g):
        rows = pl.ds(pl.multiple_of(g * step, step), step)
        return pltpu.make_async_copy(jac_hbm.at[rows], jac_v.at[rows], jac_sem.at[g])

    def ids_copy(peer, src):
        return pltpu.make_async_remote_copy(
            src_ref=ids_ref, dst_ref=ids_all.at[src], send_sem=ids_ssem.at[peer], recv_sem=ids_rsem.at[src],
            device_id=(t, peer), device_id_type=MESH)

    def block_copy(peer, src, g):
        rows = pl.ds(pl.multiple_of(g * step, step), step)
        return pltpu.make_async_remote_copy(
            src_ref=send.at[peer, rows], dst_ref=arrived.at[src, rows], send_sem=a_ssem.at[peer, g],
            recv_sem=a_rsem.at[src, g], device_id=(t, peer), device_id_type=MESH)

    def sum_copy(side, d, u, to):
        return pltpu.make_async_remote_copy(
            src_ref=dense.at[d, u], dst_ref=passing.at[side, d, u], send_sem=b_ssem.at[d, u],
            recv_sem=b_rsem.at[side, d, u], device_id=(to, o), device_id_type=MESH)

    def out_copy(peer, src, u):
        return pltpu.make_async_remote_copy(
            src_ref=stage.at[peer, u], dst_ref=fin_ref.at[src, u], send_sem=c_ssem.at[peer, u],
            recv_sem=c_rsem.at[src, u], device_id=(t, peer), device_id_type=MESH)

    each(0, groups, lambda g: jac_copy(g).start())
    barrier = pltpu.get_barrier_semaphore()
    each(1, orbits, lambda k: pl.semaphore_signal(barrier, inc=1, device_id=(t, peer_of(k)), device_id_type=MESH))

    @pl.when(t > 0)
    def _():
        pl.semaphore_signal(barrier, inc=1, device_id=(t - 1, o), device_id_type=MESH)

    @pl.when(t < tiles - 1)
    def _():
        pl.semaphore_signal(barrier, inc=1, device_id=(t + 1, o), device_id_type=MESH)

    ends = (t == 0).astype(jnp.int32) + (t == tiles - 1).astype(jnp.int32)
    pl.semaphore_wait(barrier, orbits + 1 - ends)
    each(1, orbits, lambda k: ids_copy(peer_of(k), o).start())
    ids_all[o] = ids_ref[...]

    def group(g):
        jac_copy(g).wait()
        at = pl.multiple_of(g * step, step)
        rows = pl.ds(at, step)
        coef = weights(normals_ref[:, rows, :], counts_ref[rows, :])
        flips = flip_ref[rows, :]
        for s in range(step):
            scratch[s * params : (s + 1) * params, :] = slot_block(jac_v[at + s], coef, s, flips[s : s + 1, :params])
        for unit in range(orbits * units):
            pieces = [scratch[pl.ds(unit + half * half_rows, step, stride=params), :] for half in range(2)]
            c, u = divmod(unit, units)
            send[c, rows, u * LANES : (u + 1) * LANES] = jnp.concatenate(pieces, axis=1)
        arrived[o, rows, :] = send[o, rows, :]
        each(1, orbits, lambda k: block_copy(peer_of(k), o, g).start())

    each(0, groups, group)

    each(1, orbits, lambda k: ids_copy(peer_of(k), peer_of(k)).wait_recv())

    def fill_hot(d):
        want = lax.broadcasted_iota(jnp.int32, (rank, slots), 0) + d * rank
        for p in range(orbits):
            hot[d, :, p * slots : (p + 1) * slots] = jnp.where(want == ids_all[p, 0:1, :], 1.0, 0.0).astype(jnp.bfloat16)

    each(0, tiles, fill_hot)
    each(1, orbits, lambda k: each(0, groups, lambda g: block_copy(peer_of(k), peer_of(k), g).wait_recv()))

    for u in range(units):
        found = arrived[:, :, u * LANES : (u + 1) * LANES].reshape(orbits * slots, LANES)
        high = found.astype(jnp.bfloat16)
        low = (found - high.astype(jnp.float32)).astype(jnp.bfloat16)
        halves[:, :LANES] = high
        halves[:, LANES:] = low

        def add_up(d):
            both = jnp.dot(hot[d], halves[...], preferred_element_type=jnp.float32)
            dense[d, u] = both[:, :LANES] + both[:, LANES:]

        each(0, tiles, add_up)

        @pl.when(t == 0)
        def _():
            each(1, tiles, lambda i: sum_copy(0, tiles - i, u, 1).start())

        @pl.when(t == tiles - 1)
        def _():
            each(0, tiles - 1, lambda d: sum_copy(1, d, u, tiles - 2).start())

    def finish(u):
        def relay(i):
            d = tiles - 1 - i

            @pl.when((t > 0) & (t < d))
            def _():
                sum_copy(0, d, u, t + 1).wait_recv()
                dense[d, u] = dense[d, u] + passing[0, d, u]
                sum_copy(0, d, u, t + 1).start()

            @pl.when((t < tiles - 1) & (t > i))
            def _():
                sum_copy(1, i, u, t - 1).wait_recv()
                dense[i, u] = dense[i, u] + passing[1, i, u]
                sum_copy(1, i, u, t - 1).start()

        each(0, tiles, relay)

        @pl.when(t > 0)
        def _():
            sum_copy(0, t, u, t - 1).wait_recv()
            dense[t, u] = dense[t, u] + passing[0, t, u]

        @pl.when(t < tiles - 1)
        def _():
            sum_copy(1, t, u, t + 1).wait_recv()
            dense[t, u] = dense[t, u] + passing[1, t, u]

        def hand_out(k):
            peer = peer_of(k)
            wanted = couple_ref[peer][0:1, :]
            taken = dense[t, u, 0:share, :]
            for c in range(1, orbits // 2):
                taken = jnp.where(wanted == c, dense[t, u, c * share : (c + 1) * share, :], taken)
            stage[peer, u] = taken

        each(0, orbits, hand_out)
        each(1, orbits, lambda k: out_copy(peer_of(k), o, u).start())
        pltpu.make_async_copy(stage.at[o, u], fin_ref.at[o, u], own_sem.at[u]).start()

    each(0, units, finish)

    def settle(u):
        pltpu.make_async_copy(stage.at[o, u], fin_ref.at[o, u], own_sem.at[u]).wait()
        each(1, orbits, lambda k: out_copy(peer_of(k), peer_of(k), u).wait_recv())
        each(1, orbits, lambda k: out_copy(peer_of(k), o, u).wait_send())

        def sent(d):
            @pl.when(t != d)
            def _():
                sum_copy(0, d, u, 0).wait_send()

        each(0, tiles, sent)

    each(0, units, settle)
    each(1, orbits, lambda k: ids_copy(peer_of(k), o).wait_send())
    each(1, orbits, lambda k: each(0, groups, lambda g: block_copy(peer_of(k), o, g).wait_send()))


def reduced_parts(jac, normals, counts, flip, ids, couple, orbits, tiles):
    slots, _, points, both = jac.shape
    params = both // 2
    step = min(16, slots)
    groups = slots // step
    units = params * params // LANES // orbits
    share = PAIR_ORB // tiles
    rank = orbits // 2 * share
    vmem = pl.BlockSpec(memory_space=pltpu.VMEM)
    f32 = jnp.float32
    dma = pltpu.SemaphoreType.DMA
    return pl.pallas_call(
        reduce_kernel,
        in_specs=[pl.BlockSpec(memory_space=pl.ANY), vmem, vmem, vmem, vmem, vmem],
        out_specs=pl.BlockSpec(memory_space=pl.ANY),
        out_shape=jax.ShapeDtypeStruct((orbits, units, share, LANES), f32),
        scratch_shapes=[
            pltpu.VMEM(jac.shape, jac.dtype),
            pltpu.VMEM((orbits, slots, units * LANES), f32),
            pltpu.VMEM((orbits, slots, units * LANES), f32),
            pltpu.VMEM((orbits,) + ids.shape, jnp.int32),
            pltpu.VMEM((tiles, rank, orbits * slots), jnp.bfloat16),
            pltpu.VMEM((orbits * slots, 2 * LANES), jnp.bfloat16),
            pltpu.VMEM((tiles, units, rank, LANES), f32),
            pltpu.VMEM((2, tiles, units, rank, LANES), f32),
            pltpu.VMEM((orbits, units, share, LANES), f32),
            pltpu.VMEM((step * params, params), f32),
            dma((groups,)),
            dma((orbits,)),
            dma((orbits,)),
            dma((orbits, groups)),
            dma((orbits, groups)),
            dma((tiles, units)),
            dma((2, tiles, units)),
            dma((orbits, units)),
            dma((orbits, units)),
            dma((units,)),
        ],
        compiler_params=pltpu.CompilerParams(
            collective_id=0, has_side_effects=True, vmem_limit_bytes=48 * 1024 * 1024
        ),
    )(jac, normals, counts, flip, ids, couple)


def assemble_kernel(lead_ref, fin_ref, out_ref, turned):
    count, share, _ = fin_ref.shape
    params = 2 * count
    half = LANES // 2

    @pl.when(lead_ref[0] > 0)
    def _():
        for m in range(count):
            first = (2 * m) % count
            side = (2 * m) // count * half
            out_ref[:, m * LANES : (m + 1) * LANES] = jnp.concatenate(
                [fin_ref[first + i, :, side : side + half] for i in range(2)], axis=1
            )

    @pl.when(lead_ref[0] == 0)
    def _():
        for unit in range(count):
            turned[unit * LANES : (unit + 1) * LANES, :] = jnp.transpose(fin_ref[unit])
        for m in range(count):
            rows = [turned[pl.ds(2 * m + k + h * params, count, stride=LANES), :] for k in range(2) for h in range(2)]
            out_ref[:, m * LANES : (m + 1) * LANES] = jnp.transpose(jnp.concatenate(rows, axis=0))


def assembled(lead, fin):
    count, share, _ = fin.shape
    vmem = pl.BlockSpec(memory_space=pltpu.VMEM)
    return pl.pallas_call(
        assemble_kernel,
        in_specs=[pl.BlockSpec(memory_space=pltpu.SMEM), vmem],
        out_specs=vmem,
        out_shape=jax.ShapeDtypeStruct((share, count * LANES), jnp.float32),
        scratch_shapes=[pltpu.VMEM((count * LANES, share), jnp.float32)],
        compiler_params=pltpu.CompilerParams(vmem_limit_bytes=16 * 1024 * 1024),
    )(lead, fin)


def local(jacobians, point_normals, block_counts, pair_owner, pair_local, crossing):
    slots, points, _, both = jacobians.shape
    orbits, tiles = lax.axis_size("orbit"), lax.axis_size("tile")
    couples, share = orbits // 2, PAIR_ORB // tiles
    jac = jnp.transpose(jacobians, (0, 2, 1, 3))
    normals = jnp.transpose(point_normals, (1, 0, 2))
    counts = jnp.broadcast_to(block_counts[0][:, None], (slots, points))
    orbit_ids = jnp.arange(orbits, dtype=jnp.int32)
    leads = orbit_ids < crossing
    couple = jnp.sum((orbit_ids[None, :] < jnp.minimum(orbit_ids, crossing)[:, None]) & leads[None, :], axis=1).astype(jnp.int32)
    owner_hot = pair_owner == orbit_ids[None, :]
    slot_couple = jnp.sum(jnp.where(owner_hot, couple[None, :], 0), axis=1)
    flip = jnp.sum(jnp.where(owner_hot & ~leads[None, :], 1, 0), axis=1)
    flip = jnp.broadcast_to(flip[:, None], (slots, points))
    row = (pair_local // share) * (couples * share) + slot_couple * share + pair_local % share
    ids = jnp.broadcast_to(row[None, :], (8, slots))
    wanted = jnp.broadcast_to(couple[:, None, None], (orbits, 8, LANES))
    fin = reduced_parts(jac, normals, counts, flip, ids, wanted, orbits, tiles)
    lead = leads[lax.axis_index("orbit")].astype(jnp.int32).reshape(1)
    return assembled(lead, fin.reshape(-1, share, LANES))[None]


def solution(mesh):
    in_specs = (
        P(("tile", "orbit"), None, None, None),
        P(("tile", "orbit"), None, None),
        P(("tile", "orbit"), None),
        P(("tile", "orbit"), None),
        P(("tile", "orbit")),
        P(),
    )
    out_specs = P("orbit", "tile", None)
    return jax.shard_map(local, mesh=mesh, in_specs=in_specs, out_specs=out_specs, check_vma=False)
```

```python
import jax
import jax.numpy as jnp
from jax import lax
from jax.experimental import pallas as pl
from jax.experimental.pallas import tpu as pltpu
from jax.sharding import PartitionSpec as P

PAIR_ORB = 256
LANES = 128
MESH = pl.DeviceIdType.MESH


def weights(normals, counts):
    d1, d2, d3, ab, ac, bc = (normals[i] for i in range(6))
    cof_aa = d2 * d3 - bc * bc
    cof_bb = d1 * d3 - ac * ac
    cof_cc = d1 * d2 - ab * ab
    cof_ab = ac * bc - ab * d3
    cof_ac = ab * bc - ac * d2
    cof_bc = ab * ac - d1 * bc
    det = d1 * cof_aa + ab * cof_ab + ac * cof_ac
    places = lax.broadcasted_iota(jnp.int32, det.shape, 1)
    scale = jnp.where(places < counts, 1.0, 0.0) / det
    rows = ((cof_aa, cof_ab, cof_ac), (cof_ab, cof_bb, cof_bc), (cof_ac, cof_bc, cof_cc))
    return [[entry * scale for entry in row] for row in rows]


def slot_pair(first, second, coef, s, flips):
    params, points = first.shape[-1] // 2, first.shape[-2]
    turned = [
        jnp.transpose(jnp.concatenate([first[e][:, params:], second[e][:, params:]], axis=1)).astype(jnp.float32) for e in range(3)
    ]
    mirrored = []
    for i, jac in enumerate((first, second)):
        right = [comp[i * params : (i + 1) * params] for comp in turned]
        row = slice(s + i, s + i + 1)
        solved = [
            (coef[c][0][row] * right[0] + coef[c][1][row] * right[1] + coef[c][2][row] * right[2]).astype(jnp.bfloat16)
            for c in range(3)
        ]
        block = jnp.dot(
            jnp.concatenate(solved, axis=1), jac.reshape(3 * points, 2 * params), preferred_element_type=jnp.float32
        )
        mirrored.append(block[:, :params])
    straight = jnp.transpose(jnp.concatenate(mirrored, axis=1))
    return [
        jnp.where(flips[s + i : s + i + 1, :params] > 0, mirrored[i], straight[i * params : (i + 1) * params]) for i in range(2)
    ]


def each(low, high, body):
    def step(i, carry):
        body(i)
        return carry

    lax.fori_loop(low, high, step, 0)


def reduce_kernel(
    jac_hbm, normals_ref, counts_ref, flip_ref, ids_ref, couple_ref, fin_ref,
    jac_v, send, arrived, ids_all, hot, halves, dense, passing, stage, scratch,
    jac_sem, ids_ssem, ids_rsem, a_ssem, a_rsem, b_ssem, b_rsem, c_ssem, c_rsem, own_sem,
):
    groups, cell, tiles, orbits = jac_sem.shape[0], arrived.shape[0], dense.shape[0], couple_ref.shape[0]
    units, share, rank = fin_ref.shape[1], fin_ref.shape[2], dense.shape[2]
    slots, params = jac_v.shape[0], jac_v.shape[3] // 2
    step, half_rows = slots // groups, params // 2
    near = cell // orbits
    teams = tiles // near
    t, o = lax.axis_index("tile"), lax.axis_index("orbit")
    team, seat = t // near, lax.rem(t, near)
    me = seat * orbits + o

    def peer_of(k):
        return lax.rem(me + k, cell)

    def place(member):
        return (team * near + member // orbits, lax.rem(member, orbits))

    def team_of(k):
        return lax.rem(team + k, teams)

    def jac_copy(g):
        rows = pl.ds(pl.multiple_of(g * step, step), step)
        return pltpu.make_async_copy(jac_hbm.at[rows], jac_v.at[rows], jac_sem.at[g])

    def ids_copy(peer, src):
        return pltpu.make_async_remote_copy(
            src_ref=ids_ref, dst_ref=ids_all.at[src], send_sem=ids_ssem.at[peer], recv_sem=ids_rsem.at[src],
            device_id=place(peer), device_id_type=MESH)

    def block_copy(peer, src, g):
        rows = pl.ds(pl.multiple_of(g * step, step), step)
        return pltpu.make_async_remote_copy(
            src_ref=send.at[peer, rows], dst_ref=arrived.at[src, rows], send_sem=a_ssem.at[peer, g],
            recv_sem=a_rsem.at[src, g], device_id=place(peer), device_id_type=MESH)

    def sum_copy(to, src, i, u):
        return pltpu.make_async_remote_copy(
            src_ref=dense.at[to * near + i, u], dst_ref=passing.at[src, i, u], send_sem=b_ssem.at[to, i, u],
            recv_sem=b_rsem.at[src, i, u], device_id=(to * near + seat, o), device_id_type=MESH)

    def out_copy(peer, src, u):
        return pltpu.make_async_remote_copy(
            src_ref=stage.at[peer, u], dst_ref=fin_ref.at[src, u], send_sem=c_ssem.at[peer, u],
            recv_sem=c_rsem.at[src, u], device_id=place(peer), device_id_type=MESH)

    def own_copy(u):
        return pltpu.make_async_copy(stage.at[me, u], fin_ref.at[me, u], own_sem.at[u])

    each(0, groups, lambda g: jac_copy(g).start())
    barrier = pltpu.get_barrier_semaphore()
    each(1, cell, lambda k: pl.semaphore_signal(barrier, inc=1, device_id=place(peer_of(k)), device_id_type=MESH))
    each(1, teams, lambda k: pl.semaphore_signal(
        barrier, inc=1, device_id=(team_of(k) * near + seat, o), device_id_type=MESH))
    pl.semaphore_wait(barrier, cell - 1 + teams - 1)

    each(1, cell, lambda k: ids_copy(peer_of(k), me).start())
    ids_all[me] = ids_ref[...]

    def group(g):
        jac_copy(g).wait()
        at = pl.multiple_of(g * step, step)
        rows = pl.ds(at, step)
        coef = weights(normals_ref[:, rows, :], counts_ref[rows, :])
        flips = flip_ref[rows, :]
        for s in range(0, step, 2):
            for i, block in enumerate(slot_pair(jac_v[at + s], jac_v[at + s + 1], coef, s, flips)):
                scratch[(s + i) * params : (s + i + 1) * params, :] = block
        for unit in range(cell * units):
            pieces = [scratch[pl.ds(unit + half * half_rows, step, stride=params), :] for half in range(2)]
            c, u = divmod(unit, units)
            send[c, rows, u * LANES : (u + 1) * LANES] = jnp.concatenate(pieces, axis=1)
        arrived[me, rows, :] = send[me, rows, :]
        each(1, cell, lambda k: block_copy(peer_of(k), me, g).start())

    each(0, groups, group)

    each(1, cell, lambda k: ids_copy(peer_of(k), peer_of(k)).wait_recv())

    def fill_hot(d):
        want = lax.broadcasted_iota(jnp.int32, (rank, slots), 0) + d * rank
        for p in range(cell):
            hot[d, :, p * slots : (p + 1) * slots] = jnp.where(want == ids_all[p, 0:1, :], 1.0, 0.0).astype(jnp.bfloat16)

    each(0, tiles, fill_hot)
    each(1, cell, lambda k: each(0, groups, lambda g: block_copy(peer_of(k), peer_of(k), g).wait_recv()))

    def add_up(d, u):
        both = jnp.dot(hot[d], halves[u], preferred_element_type=jnp.float32)
        dense[d, u] = both[:, :LANES] + both[:, LANES:]

    for u in range(units):
        found = arrived[:, :, u * LANES : (u + 1) * LANES].reshape(cell * slots, LANES)
        high = found.astype(jnp.bfloat16)
        low = (found - high.astype(jnp.float32)).astype(jnp.bfloat16)
        halves[u, :, :LANES] = high
        halves[u, :, LANES:] = low

        def away(n):
            to, i = team_of(1 + n // near), lax.rem(n, near)
            add_up(to * near + i, u)
            sum_copy(to, team, i, u).start()

        each(0, (teams - 1) * near, away)

    each(0, units, lambda u: each(0, near, lambda i: add_up(team * near + i, u)))

    def finish(n):
        u, i = n // near, lax.rem(n, near)
        d = team * near + i

        def gather_in(k):
            src = team_of(k)
            sum_copy(src, src, i, u).wait_recv()
            dense[d, u] = dense[d, u] + passing[src, i, u]

        each(1, teams, gather_in)

        def hand_out(k):
            member = i * orbits + k
            wanted = couple_ref[k][0:1, :]
            taken = dense[d, u, 0:share, :]
            for c in range(1, orbits // 2):
                taken = jnp.where(wanted == c, dense[d, u, c * share : (c + 1) * share, :], taken)
            stage[member, u] = taken

            @pl.when(member != me)
            def _():
                out_copy(member, me, u).start()

            @pl.when(member == me)
            def _():
                own_copy(u).start()

        each(0, orbits, hand_out)

    each(0, units * near, finish)

    def settle(u):
        own_copy(u).wait()
        each(1, cell, lambda k: out_copy(peer_of(k), peer_of(k), u).wait_recv())
        each(1, cell, lambda k: out_copy(peer_of(k), me, u).wait_send())
        each(1, teams, lambda k: each(0, near, lambda i: sum_copy(team_of(k), team, i, u).wait_send()))

    each(0, units, settle)
    each(1, cell, lambda k: ids_copy(peer_of(k), me).wait_send())
    each(1, cell, lambda k: each(0, groups, lambda g: block_copy(peer_of(k), me, g).wait_send()))


def reduced_parts(jac, normals, counts, flip, ids, couple, orbits, tiles):
    slots, _, points, both = jac.shape
    params = both // 2
    step = min(16, slots)
    groups = slots // step
    near = 2 if tiles % 2 == 0 and params * params % (2 * orbits * LANES) == 0 else 1
    cell, teams = near * orbits, tiles // near
    units = params * params // LANES // cell
    share = PAIR_ORB // tiles
    rank = orbits // 2 * share
    vmem = pl.BlockSpec(memory_space=pltpu.VMEM)
    f32 = jnp.float32
    dma = pltpu.SemaphoreType.DMA
    return pl.pallas_call(
        reduce_kernel,
        in_specs=[pl.BlockSpec(memory_space=pl.ANY), vmem, vmem, vmem, vmem, vmem],
        out_specs=pl.BlockSpec(memory_space=pl.ANY),
        out_shape=jax.ShapeDtypeStruct((cell, units, share, LANES), f32),
        scratch_shapes=[
            pltpu.VMEM(jac.shape, jac.dtype),
            pltpu.VMEM((cell, slots, units * LANES), f32),
            pltpu.VMEM((cell, slots, units * LANES), f32),
            pltpu.VMEM((cell,) + ids.shape, jnp.int32),
            pltpu.VMEM((tiles, rank, cell * slots), jnp.bfloat16),
            pltpu.VMEM((units, cell * slots, 2 * LANES), jnp.bfloat16),
            pltpu.VMEM((tiles, units, rank, LANES), f32),
            pltpu.VMEM((teams, near, units, rank, LANES), f32),
            pltpu.VMEM((cell, units, share, LANES), f32),
            pltpu.VMEM((step * params, params), f32),
            dma((groups,)),
            dma((cell,)),
            dma((cell,)),
            dma((cell, groups)),
            dma((cell, groups)),
            dma((teams, near, units)),
            dma((teams, near, units)),
            dma((cell, units)),
            dma((cell, units)),
            dma((units,)),
        ],
        compiler_params=pltpu.CompilerParams(
            collective_id=0, has_side_effects=True, vmem_limit_bytes=48 * 1024 * 1024
        ),
    )(jac, normals, counts, flip, ids, couple)


def assemble_kernel(lead_ref, fin_ref, out_ref, turned):
    count, share, _ = fin_ref.shape
    params = 2 * count
    half = LANES // 2

    @pl.when(lead_ref[0] > 0)
    def _():
        for m in range(count):
            first = (2 * m) % count
            side = (2 * m) // count * half
            out_ref[:, m * LANES : (m + 1) * LANES] = jnp.concatenate(
                [fin_ref[first + i, :, side : side + half] for i in range(2)], axis=1
            )

    @pl.when(lead_ref[0] == 0)
    def _():
        for unit in range(count):
            turned[unit * LANES : (unit + 1) * LANES, :] = jnp.transpose(fin_ref[unit])
        for m in range(count):
            rows = [turned[pl.ds(2 * m + k + h * params, count, stride=LANES), :] for k in range(2) for h in range(2)]
            out_ref[:, m * LANES : (m + 1) * LANES] = jnp.transpose(jnp.concatenate(rows, axis=0))


def assembled(lead, fin):
    count, share, _ = fin.shape
    vmem = pl.BlockSpec(memory_space=pltpu.VMEM)
    return pl.pallas_call(
        assemble_kernel,
        in_specs=[pl.BlockSpec(memory_space=pltpu.SMEM), vmem],
        out_specs=vmem,
        out_shape=jax.ShapeDtypeStruct((share, count * LANES), jnp.float32),
        scratch_shapes=[pltpu.VMEM((count * LANES, share), jnp.float32)],
        compiler_params=pltpu.CompilerParams(vmem_limit_bytes=16 * 1024 * 1024),
    )(lead, fin)


def local(jacobians, point_normals, block_counts, pair_owner, pair_local, crossing):
    slots, points, _, both = jacobians.shape
    orbits, tiles = lax.axis_size("orbit"), lax.axis_size("tile")
    couples, share = orbits // 2, PAIR_ORB // tiles
    jac = jnp.transpose(jacobians, (0, 2, 1, 3))
    normals = jnp.transpose(point_normals, (1, 0, 2))
    counts = jnp.broadcast_to(block_counts[0][:, None], (slots, points))
    orbit_ids = jnp.arange(orbits, dtype=jnp.int32)
    leads = orbit_ids < crossing
    couple = jnp.sum((orbit_ids[None, :] < jnp.minimum(orbit_ids, crossing)[:, None]) & leads[None, :], axis=1).astype(jnp.int32)
    owner_hot = pair_owner == orbit_ids[None, :]
    slot_couple = jnp.sum(jnp.where(owner_hot, couple[None, :], 0), axis=1)
    flip = jnp.sum(jnp.where(owner_hot & ~leads[None, :], 1, 0), axis=1)
    flip = jnp.broadcast_to(flip[:, None], (slots, points))
    row = (pair_local // share) * (couples * share) + slot_couple * share + pair_local % share
    ids = jnp.broadcast_to(row[None, :], (8, slots))
    wanted = jnp.broadcast_to(couple[:, None, None], (orbits, 8, LANES))
    fin = reduced_parts(jac, normals, counts, flip, ids, wanted, orbits, tiles)
    lead = leads[lax.axis_index("orbit")].astype(jnp.int32).reshape(1)
    return assembled(lead, fin.reshape(-1, share, LANES))[None]


def solution(mesh):
    in_specs = (
        P(("tile", "orbit"), None, None, None),
        P(("tile", "orbit"), None, None),
        P(("tile", "orbit"), None),
        P(("tile", "orbit"), None),
        P(("tile", "orbit")),
        P(),
    )
    out_specs = P("orbit", "tile", None)
    return jax.shard_map(local, mesh=mesh, in_specs=in_specs, out_specs=out_specs, check_vma=False)
```

```python
import jax
import jax.numpy as jnp
from jax import lax
from jax.experimental import pallas as pl
from jax.experimental.pallas import tpu as pltpu
from jax.sharding import PartitionSpec as P

PAIR_ORB = 256
LANES = 128
MESH = pl.DeviceIdType.MESH


def weights(normals, counts):
    d1, d2, d3, ab, ac, bc = (normals[i] for i in range(6))
    cof_aa = d2 * d3 - bc * bc
    cof_bb = d1 * d3 - ac * ac
    cof_cc = d1 * d2 - ab * ab
    cof_ab = ac * bc - ab * d3
    cof_ac = ab * bc - ac * d2
    cof_bc = ab * ac - d1 * bc
    det = d1 * cof_aa + ab * cof_ab + ac * cof_ac
    places = lax.broadcasted_iota(jnp.int32, det.shape, 1).astype(jnp.float32)
    scale = jnp.where(places < counts, 1.0, 0.0) / det
    rows = ((cof_aa, cof_ab, cof_ac), (cof_ab, cof_bb, cof_bc), (cof_ac, cof_bc, cof_cc))
    return [[entry * scale for entry in row] for row in rows]


def slot_pair(first, second, coef, s, flips):
    params, points = first.shape[-1] // 2, first.shape[-2]
    turned = [
        jnp.transpose(jnp.concatenate([first[e][:, params:], second[e][:, params:]], axis=1)).astype(jnp.float32) for e in range(3)
    ]
    mirrored = []
    for i, jac in enumerate((first, second)):
        right = [comp[i * params : (i + 1) * params] for comp in turned]
        row = slice(s + i, s + i + 1)
        solved = [
            (coef[c][0][row] * right[0] + coef[c][1][row] * right[1] + coef[c][2][row] * right[2]).astype(jnp.bfloat16)
            for c in range(3)
        ]
        block = jnp.dot(
            jnp.concatenate(solved, axis=1), jac.reshape(3 * points, 2 * params), preferred_element_type=jnp.float32
        )
        mirrored.append(block[:, :params])
    straight = jnp.transpose(jnp.concatenate(mirrored, axis=1))
    return [
        jnp.where(flips[s + i : s + i + 1, :params] > 0, mirrored[i], straight[i * params : (i + 1) * params]) for i in range(2)
    ]


def each(low, high, body):
    def step(i, carry):
        body(i)
        return carry

    lax.fori_loop(low, high, step, 0)


def reduce_kernel(
    jac_hbm, normals_hbm, counts_ref, owner_ref, local_ref, crossing_ref, fin_ref,
    normals_v, counts_v, flip_v, ids_v, couple_v, jac_v, send, arrived, ids_all, hot, halves, dense, passing, stage, scratch,
    normals_sem, jac_sem, ids_ssem, ids_rsem, a_ssem, a_rsem, b_ssem, b_rsem, c_ssem, c_rsem, own_sem,
):
    groups, cell, tiles, orbits = jac_sem.shape[0], arrived.shape[0], dense.shape[0], crossing_ref.shape[0]
    units, share, rank = fin_ref.shape[1], fin_ref.shape[2], dense.shape[2]
    slots, params = jac_v.shape[0], jac_v.shape[3] // 2
    step, half_rows = slots // groups, params // 2
    near = cell // orbits
    teams = tiles // near
    t, o = lax.axis_index("tile"), lax.axis_index("orbit")
    team, seat = t // near, lax.rem(t, near)
    me = seat * orbits + o

    def peer_of(k):
        return lax.rem(me + k, cell)

    def place(member):
        return (team * near + member // orbits, lax.rem(member, orbits))

    def team_of(k):
        return lax.rem(team + k, teams)

    def jac_copy(g):
        rows = pl.ds(pl.multiple_of(g * step, step), step)
        return pltpu.make_async_copy(jac_hbm.at[rows], jac_v.at[rows], jac_sem.at[g])

    def ids_copy(peer, src):
        return pltpu.make_async_remote_copy(
            src_ref=ids_v, dst_ref=ids_all.at[src], send_sem=ids_ssem.at[peer], recv_sem=ids_rsem.at[src],
            device_id=place(peer), device_id_type=MESH)

    def block_copy(peer, src, g):
        rows = pl.ds(pl.multiple_of(g * step, step), step)
        return pltpu.make_async_remote_copy(
            src_ref=send.at[peer, rows], dst_ref=arrived.at[src, rows], send_sem=a_ssem.at[peer, g],
            recv_sem=a_rsem.at[src, g], device_id=place(peer), device_id_type=MESH)

    def sum_copy(to, src, i, u):
        return pltpu.make_async_remote_copy(
            src_ref=dense.at[to * near + i, u], dst_ref=passing.at[src, i, u], send_sem=b_ssem.at[to, i, u],
            recv_sem=b_rsem.at[src, i, u], device_id=(to * near + seat, o), device_id_type=MESH)

    def out_copy(peer, src, u):
        return pltpu.make_async_remote_copy(
            src_ref=stage.at[peer, u], dst_ref=fin_ref.at[src, u], send_sem=c_ssem.at[peer, u],
            recv_sem=c_rsem.at[src, u], device_id=place(peer), device_id_type=MESH)

    def own_copy(u):
        return pltpu.make_async_copy(stage.at[me, u], fin_ref.at[me, u], own_sem.at[u])

    normals_copy = pltpu.make_async_copy(normals_hbm, normals_v, normals_sem)
    normals_copy.start()
    each(0, groups, lambda g: jac_copy(g).start())
    barrier = pltpu.get_barrier_semaphore()
    each(1, cell, lambda k: pl.semaphore_signal(barrier, inc=1, device_id=place(peer_of(k)), device_id_type=MESH))
    each(1, teams, lambda k: pl.semaphore_signal(
        barrier, inc=1, device_id=(team_of(k) * near + seat, o), device_id_type=MESH))

    points = normals_v.shape[2]
    lead = [(k < crossing_ref[k]).astype(jnp.int32) for k in range(orbits)]
    first = [jnp.minimum(k, crossing_ref[k]) for k in range(orbits)]
    couple = [sum(lead[j] * (j < first[k]).astype(jnp.int32) for j in range(orbits)) for k in range(orbits)]
    owner = jnp.broadcast_to(owner_ref[...], ids_v.shape)
    where = jnp.broadcast_to(local_ref[...], ids_v.shape)
    slot_couple, slot_flip, slot_tile = (jnp.zeros(ids_v.shape, jnp.int32) for _ in range(3))
    for k in range(orbits):
        hit = (owner == k).astype(jnp.int32)
        slot_couple = slot_couple + hit * couple[k]
        slot_flip = slot_flip + hit * (1 - lead[k])
        couple_v[k] = jnp.full(couple_v.shape[1:], couple[k], jnp.int32)
    for d in range(1, tiles):
        slot_tile = slot_tile + (where >= d * share).astype(jnp.int32)
    ids_v[...] = slot_tile * rank + slot_couple * share + where - slot_tile * share
    for column, row in ((flip_v, slot_flip[0:1]), (counts_v, counts_ref[...])):
        column[...] = jnp.transpose(jnp.broadcast_to(row.astype(jnp.float32), (points, slots)))

    pl.semaphore_wait(barrier, cell - 1 + teams - 1)

    each(1, cell, lambda k: ids_copy(peer_of(k), me).start())
    ids_all[me] = ids_v[...]
    normals_copy.wait()

    def group(g):
        jac_copy(g).wait()
        at = pl.multiple_of(g * step, step)
        rows = pl.ds(at, step)
        coef = weights(normals_v[:, rows, :], counts_v[rows, :])
        flips = flip_v[rows, :]
        for s in range(0, step, 2):
            for i, block in enumerate(slot_pair(jac_v[at + s], jac_v[at + s + 1], coef, s, flips)):
                scratch[(s + i) * params : (s + i + 1) * params, :] = block
        for unit in range(cell * units):
            pieces = [scratch[pl.ds(unit + half * half_rows, step, stride=params), :] for half in range(2)]
            c, u = divmod(unit, units)
            send[c, rows, u * LANES : (u + 1) * LANES] = jnp.concatenate(pieces, axis=1)
        arrived[me, rows, :] = send[me, rows, :]
        each(1, cell, lambda k: block_copy(peer_of(k), me, g).start())

    each(0, groups, group)

    each(1, cell, lambda k: ids_copy(peer_of(k), peer_of(k)).wait_recv())

    def fill_hot(who, i):
        rows = slice(i * rank, (i + 1) * rank)
        want = lax.broadcasted_iota(jnp.int32, (rank, slots), 0) + (who * near + i) * rank
        for p in range(cell):
            hot[who, rows, p * slots : (p + 1) * slots] = jnp.where(want == ids_all[p, 0:1, :], 1.0, 0.0).astype(jnp.bfloat16)

    def fill_team(k):
        for i in range(near):
            fill_hot(team_of(k), i)

    each(1, teams, fill_team)
    each(1, cell, lambda k: each(0, groups, lambda g: block_copy(peer_of(k), peer_of(k), g).wait_recv()))

    def add_up(who, u):
        both = jnp.dot(hot[who], halves[u], preferred_element_type=jnp.float32)
        both = both[:, :LANES] + both[:, LANES:]
        for i in range(near):
            dense[who * near + i, u] = both[i * rank : (i + 1) * rank]

    for u in range(units):
        found = arrived[:, :, u * LANES : (u + 1) * LANES].reshape(cell * slots, LANES)
        high = found.astype(jnp.bfloat16)
        low = (found - high.astype(jnp.float32)).astype(jnp.bfloat16)
        halves[u, :, :LANES] = high
        halves[u, :, LANES:] = low

        def away(k):
            add_up(team_of(k), u)
            each(0, near, lambda i: sum_copy(team_of(k), team, i, u).start())

        each(1, teams, away)

    fill_team(0)
    each(0, units, lambda u: add_up(team, u))

    def finish(n):
        u, i = n // near, lax.rem(n, near)
        d = team * near + i

        def gather_in(k):
            src = team_of(k)
            sum_copy(src, src, i, u).wait_recv()
            dense[d, u] = dense[d, u] + passing[src, i, u]

        each(1, teams, gather_in)

        def hand_out(k):
            member = i * orbits + k
            wanted = couple_v[k][0:1, :]
            taken = dense[d, u, 0:share, :]
            for c in range(1, orbits // 2):
                taken = jnp.where(wanted == c, dense[d, u, c * share : (c + 1) * share, :], taken)
            stage[member, u] = taken

            @pl.when(member != me)
            def _():
                out_copy(member, me, u).start()

            @pl.when(member == me)
            def _():
                own_copy(u).start()

        each(0, orbits, hand_out)

    each(0, units * near, finish)

    def settle(u):
        own_copy(u).wait()
        each(1, cell, lambda k: out_copy(peer_of(k), peer_of(k), u).wait_recv())
        each(1, cell, lambda k: out_copy(peer_of(k), me, u).wait_send())
        each(1, teams, lambda k: each(0, near, lambda i: sum_copy(team_of(k), team, i, u).wait_send()))

    each(0, units, settle)
    each(1, cell, lambda k: ids_copy(peer_of(k), me).wait_send())
    each(1, cell, lambda k: each(0, groups, lambda g: block_copy(peer_of(k), me, g).wait_send()))


def reduced_parts(jac, normals, counts, owner, where, crossing, tiles):
    slots, _, points, both = jac.shape
    orbits = crossing.shape[0]
    params = both // 2
    step = min(16, slots)
    groups = slots // step
    near = 2 if tiles % 2 == 0 and params * params % (2 * orbits * LANES) == 0 else 1
    cell, teams = near * orbits, tiles // near
    units = params * params // LANES // cell
    share = PAIR_ORB // tiles
    rank = orbits // 2 * share
    vmem = pl.BlockSpec(memory_space=pltpu.VMEM)
    f32 = jnp.float32
    dma = pltpu.SemaphoreType.DMA
    return pl.pallas_call(
        reduce_kernel,
        in_specs=[pl.BlockSpec(memory_space=pl.ANY)] * 2 + [vmem] * 3 + [pl.BlockSpec(memory_space=pltpu.SMEM)],
        out_specs=pl.BlockSpec(memory_space=pl.ANY),
        out_shape=jax.ShapeDtypeStruct((cell, units, share, LANES), f32),
        scratch_shapes=[
            pltpu.VMEM(normals.shape, f32),
            pltpu.VMEM((slots, points), f32),
            pltpu.VMEM((slots, points), f32),
            pltpu.VMEM((8, slots), jnp.int32),
            pltpu.VMEM((orbits, 8, LANES), jnp.int32),
            pltpu.VMEM(jac.shape, jac.dtype),
            pltpu.VMEM((cell, slots, units * LANES), f32),
            pltpu.VMEM((cell, slots, units * LANES), f32),
            pltpu.VMEM((cell, 8, slots), jnp.int32),
            pltpu.VMEM((teams, near * rank, cell * slots), jnp.bfloat16),
            pltpu.VMEM((units, cell * slots, 2 * LANES), jnp.bfloat16),
            pltpu.VMEM((tiles, units, rank, LANES), f32),
            pltpu.VMEM((teams, near, units, rank, LANES), f32),
            pltpu.VMEM((cell, units, share, LANES), f32),
            pltpu.VMEM((step * params, params), f32),
            pltpu.SemaphoreType.DMA,
            dma((groups,)),
            dma((cell,)),
            dma((cell,)),
            dma((cell, groups)),
            dma((cell, groups)),
            dma((teams, near, units)),
            dma((teams, near, units)),
            dma((cell, units)),
            dma((cell, units)),
            dma((units,)),
        ],
        compiler_params=pltpu.CompilerParams(
            collective_id=0, has_side_effects=True, vmem_limit_bytes=48 * 1024 * 1024
        ),
    )(jac, normals, counts, owner, where, crossing)


def assemble_kernel(crossing_ref, fin_ref, out_ref, turned):
    orbit = lax.axis_index("orbit")
    leads = crossing_ref[orbit] > orbit
    count, share, _ = fin_ref.shape
    params = 2 * count
    half = LANES // 2

    @pl.when(leads)
    def _():
        for m in range(count):
            first = (2 * m) % count
            side = (2 * m) // count * half
            out_ref[:, m * LANES : (m + 1) * LANES] = jnp.concatenate(
                [fin_ref[first + i, :, side : side + half] for i in range(2)], axis=1
            )

    @pl.when(jnp.logical_not(leads))
    def _():
        for unit in range(count):
            turned[unit * LANES : (unit + 1) * LANES, :] = jnp.transpose(fin_ref[unit])
        for m in range(count):
            rows = [turned[pl.ds(2 * m + k + h * params, count, stride=LANES), :] for k in range(2) for h in range(2)]
            out_ref[:, m * LANES : (m + 1) * LANES] = jnp.transpose(jnp.concatenate(rows, axis=0))


def assembled(crossing, fin):
    count, share, _ = fin.shape
    vmem = pl.BlockSpec(memory_space=pltpu.VMEM)
    return pl.pallas_call(
        assemble_kernel,
        in_specs=[pl.BlockSpec(memory_space=pltpu.SMEM), vmem],
        out_specs=vmem,
        out_shape=jax.ShapeDtypeStruct((share, count * LANES), jnp.float32),
        scratch_shapes=[pltpu.VMEM((count * LANES, share), jnp.float32)],
        compiler_params=pltpu.CompilerParams(vmem_limit_bytes=16 * 1024 * 1024),
    )(crossing, fin)


def local(jacobians, point_normals, block_counts, pair_owner, pair_local, crossing):
    tiles = lax.axis_size("tile")
    jac = jnp.transpose(jacobians, (0, 2, 1, 3))
    normals = jnp.transpose(point_normals, (1, 0, 2))
    owner, where = pair_owner.reshape(1, -1), pair_local.reshape(1, -1)
    fin = reduced_parts(jac, normals, block_counts, owner, where, crossing, tiles)
    return assembled(crossing, fin.reshape(-1, PAIR_ORB // tiles, LANES))[None]


def solution(mesh):
    in_specs = (
        P(("tile", "orbit"), None, None, None),
        P(("tile", "orbit"), None, None),
        P(("tile", "orbit"), None),
        P(("tile", "orbit"), None),
        P(("tile", "orbit")),
        P(),
    )
    out_specs = P("orbit", "tile", None)
    return jax.shard_map(local, mesh=mesh, in_specs=in_specs, out_specs=out_specs, check_vma=False)
```

```python
import jax
import jax.numpy as jnp
from jax import lax
from jax.experimental import pallas as pl
from jax.experimental.pallas import tpu as pltpu
from jax.sharding import PartitionSpec as P

PAIR_ORB = 256
LANES = 128
MESH = pl.DeviceIdType.MESH


def weights(normals, counts):
    d1, d2, d3, ab, ac, bc = (normals[i] for i in range(6))
    cof_aa = d2 * d3 - bc * bc
    cof_bb = d1 * d3 - ac * ac
    cof_cc = d1 * d2 - ab * ab
    cof_ab = ac * bc - ab * d3
    cof_ac = ab * bc - ac * d2
    cof_bc = ab * ac - d1 * bc
    det = d1 * cof_aa + ab * cof_ab + ac * cof_ac
    places = lax.broadcasted_iota(jnp.int32, det.shape, 1).astype(jnp.float32)
    scale = jnp.where(places < counts, 1.0, 0.0) / det
    rows = ((cof_aa, cof_ab, cof_ac), (cof_ab, cof_bb, cof_bc), (cof_ac, cof_bc, cof_cc))
    return [[entry * scale for entry in row] for row in rows]


def slot_pair(first, second, coef, s, flips):
    params, points = first.shape[-1] // 2, first.shape[-2]
    turned = [
        jnp.transpose(jnp.concatenate([first[e][:, params:], second[e][:, params:]], axis=1)).astype(jnp.float32) for e in range(3)
    ]
    mirrored = []
    for i, jac in enumerate((first, second)):
        right = [comp[i * params : (i + 1) * params] for comp in turned]
        row = slice(s + i, s + i + 1)
        solved = [
            (coef[c][0][row] * right[0] + coef[c][1][row] * right[1] + coef[c][2][row] * right[2]).astype(jnp.bfloat16)
            for c in range(3)
        ]
        block = jnp.dot(
            jnp.concatenate(solved, axis=1), jac.reshape(3 * points, 2 * params), preferred_element_type=jnp.float32
        )
        mirrored.append(block[:, :params])
    straight = jnp.transpose(jnp.concatenate(mirrored, axis=1))
    return [
        jnp.where(flips[s + i : s + i + 1, :params] > 0, mirrored[i], straight[i * params : (i + 1) * params]) for i in range(2)
    ]


def each(low, high, body):
    def step(i, carry):
        body(i)
        return carry

    lax.fori_loop(low, high, step, 0)


def reduce_kernel(
    jac_hbm, normals_hbm, counts_hbm, owner_hbm, local_hbm, crossing_ref, fin_ref,
    counts_ref, owner_ref, local_ref, normals_v, counts_v, flip_v, ids_v, couple_v, jac_v, send, arrived, ids_all, hot, halves, dense, passing, stage, scratch,
    small_sem, normals_sem, jac_sem, ids_ssem, ids_rsem, a_ssem, a_rsem, b_ssem, b_rsem, c_ssem, c_rsem, own_sem,
):
    groups, cell, tiles, orbits = jac_sem.shape[0], arrived.shape[1], dense.shape[0], crossing_ref.shape[0]
    units, share, rank = fin_ref.shape[1], fin_ref.shape[2], dense.shape[2]
    slots, params = jac_v.shape[0], jac_v.shape[3] // 2
    step, half_rows = slots // groups, params // 2
    batches = max(1, groups // 2)
    batch = slots // batches
    near = cell // orbits
    teams = tiles // near
    t, o = lax.axis_index("tile"), lax.axis_index("orbit")
    team, seat = t // near, lax.rem(t, near)
    me = seat * orbits + o

    def peer_of(k):
        return lax.rem(me + k, cell)

    def place(member):
        return (team * near + member // orbits, lax.rem(member, orbits))

    def team_of(k):
        return lax.rem(team + k, teams)

    def jac_copy(g):
        rows = pl.ds(pl.multiple_of(g * step, step), step)
        return pltpu.make_async_copy(jac_hbm.at[rows], jac_v.at[rows], jac_sem.at[g])

    def ids_copy(peer, src):
        return pltpu.make_async_remote_copy(
            src_ref=ids_v, dst_ref=ids_all.at[src], send_sem=ids_ssem.at[peer], recv_sem=ids_rsem.at[src],
            device_id=place(peer), device_id_type=MESH)

    def block_copy(peer, src, u, rows):
        return pltpu.make_async_remote_copy(
            src_ref=send.at[u, peer, rows], dst_ref=arrived.at[u, src, rows], send_sem=a_ssem.at[u, peer],
            recv_sem=a_rsem.at[u, src], device_id=place(peer), device_id_type=MESH)

    whole_slots = pl.ds(0, slots)

    def send_batch(u, n):
        rows = pl.ds(pl.multiple_of(n * batch, batch), batch)
        each(1, cell, lambda k: block_copy(peer_of(k), me, u, rows).start())

    def sum_copy(to, src, i, u):
        return pltpu.make_async_remote_copy(
            src_ref=dense.at[to * near + i, u], dst_ref=passing.at[src, i, u], send_sem=b_ssem.at[to, i, u],
            recv_sem=b_rsem.at[src, i, u], device_id=(to * near + seat, o), device_id_type=MESH)

    def out_copy(peer, src, u):
        return pltpu.make_async_remote_copy(
            src_ref=stage.at[peer, u], dst_ref=fin_ref.at[src, u], send_sem=c_ssem.at[peer, u],
            recv_sem=c_rsem.at[src, u], device_id=place(peer), device_id_type=MESH)

    def own_copy(u):
        return pltpu.make_async_copy(stage.at[me, u], fin_ref.at[me, u], own_sem.at[u])

    normals_copy = pltpu.make_async_copy(normals_hbm, normals_v, normals_sem)
    small = [
        pltpu.make_async_copy(src, dst, small_sem.at[i])
        for i, (src, dst) in enumerate(((counts_hbm, counts_ref), (owner_hbm, owner_ref), (local_hbm, local_ref)))
    ]
    for copy in small:
        copy.start()
    normals_copy.start()
    each(0, groups, lambda g: jac_copy(g).start())
    barrier = pltpu.get_barrier_semaphore()
    each(1, cell, lambda k: pl.semaphore_signal(barrier, inc=1, device_id=place(peer_of(k)), device_id_type=MESH))
    each(1, teams, lambda k: pl.semaphore_signal(
        barrier, inc=1, device_id=(team_of(k) * near + seat, o), device_id_type=MESH))

    points = normals_v.shape[2]
    lead = [(k < crossing_ref[k]).astype(jnp.int32) for k in range(orbits)]
    first = [jnp.minimum(k, crossing_ref[k]) for k in range(orbits)]
    couple = [sum(lead[j] * (j < first[k]).astype(jnp.int32) for j in range(orbits)) for k in range(orbits)]
    for copy in small:
        copy.wait()
    owner = jnp.broadcast_to(owner_ref[...], ids_v.shape)
    where = jnp.broadcast_to(local_ref[...], ids_v.shape)
    slot_couple, slot_flip, slot_tile = (jnp.zeros(ids_v.shape, jnp.int32) for _ in range(3))
    for k in range(orbits):
        hit = (owner == k).astype(jnp.int32)
        slot_couple = slot_couple + hit * couple[k]
        slot_flip = slot_flip + hit * (1 - lead[k])
        couple_v[k] = jnp.full(couple_v.shape[1:], couple[k], jnp.int32)
    for d in range(1, tiles):
        slot_tile = slot_tile + (where >= d * share).astype(jnp.int32)
    ids_v[...] = slot_tile * rank + slot_couple * share + where - slot_tile * share
    for column, row in ((flip_v, slot_flip[0:1]), (counts_v, counts_ref[...])):
        column[...] = jnp.transpose(jnp.broadcast_to(row.astype(jnp.float32), (points, slots)))

    pl.semaphore_wait(barrier, cell - 1 + teams - 1)

    each(1, cell, lambda k: ids_copy(peer_of(k), me).start())
    ids_all[me] = ids_v[...]
    normals_copy.wait()

    def group(g):
        jac_copy(g).wait()
        at = pl.multiple_of(g * step, step)
        rows = pl.ds(at, step)
        coef = weights(normals_v[:, rows, :], counts_v[rows, :])
        flips = flip_v[rows, :]
        for s in range(0, step, 2):
            for i, block in enumerate(slot_pair(jac_v[at + s], jac_v[at + s + 1], coef, s, flips)):
                scratch[(s + i) * params : (s + i + 1) * params, :] = block
        for unit in range(cell * units):
            pieces = [scratch[pl.ds(unit + half * half_rows, step, stride=params), :] for half in range(2)]
            c, u = divmod(unit, units)
            send[u, c, rows, :] = jnp.concatenate(pieces, axis=1)
        for u in range(units):
            arrived[u, me, rows, :] = send[u, me, rows, :]

    early = batches // 2

    def run_batch(n):
        each(n * (groups // batches), (n + 1) * (groups // batches), group)
        send_batch(0, n)

        @pl.when(n < early)
        def _():
            for u in range(1, units):
                send_batch(u, n)

    each(0, batches, run_batch)
    for u in range(1, units):
        each(early, batches, lambda n: send_batch(u, n))

    each(1, cell, lambda k: ids_copy(peer_of(k), peer_of(k)).wait_recv())

    def fill_hot(who, i):
        want = lax.broadcasted_iota(jnp.int32, (rank, slots), 0) + (who * near + i) * rank
        for p in range(cell):
            hot[who, i, :, p * slots : (p + 1) * slots] = jnp.where(want == ids_all[p, 0:1, :], 1.0, 0.0).astype(jnp.bfloat16)

    def fill_team(k):
        for i in range(near):
            fill_hot(team_of(k), i)

    each(1, teams, fill_team)

    def add_up(who, i, u):
        both = jnp.dot(hot[who, i], halves[u], preferred_element_type=jnp.float32)
        dense[who * near + i, u] = both[:, :LANES] + both[:, LANES:]

    for u in range(units):
        each(1, cell, lambda k: block_copy(peer_of(k), peer_of(k), u, whole_slots).wait_recv())
        found = arrived[u].reshape(cell * slots, LANES)
        high = found.astype(jnp.bfloat16)
        low = (found - high.astype(jnp.float32)).astype(jnp.bfloat16)
        halves[u, :, :LANES] = high
        halves[u, :, LANES:] = low

        def away(n):
            to, i = team_of(1 + n // near), lax.rem(n, near)
            add_up(to, i, u)
            sum_copy(to, team, i, u).start()

        each(0, (teams - 1) * near, away)

    fill_team(0)
    each(0, units, lambda u: each(0, near, lambda i: add_up(team, i, u)))

    def finish(n):
        u, i = n // near, lax.rem(n, near)
        d = team * near + i

        def gather_in(k):
            src = team_of(k)
            sum_copy(src, src, i, u).wait_recv()
            dense[d, u] = dense[d, u] + passing[src, i, u]

        each(1, teams, gather_in)

        def hand_out(k):
            member = i * orbits + k
            wanted = couple_v[k][0:1, :]
            taken = dense[d, u, 0:share, :]
            for c in range(1, orbits // 2):
                taken = jnp.where(wanted == c, dense[d, u, c * share : (c + 1) * share, :], taken)
            stage[member, u] = taken

            @pl.when(member != me)
            def _():
                out_copy(member, me, u).start()

            @pl.when(member == me)
            def _():
                own_copy(u).start()

        each(0, orbits, hand_out)

    each(0, units * near, finish)

    def settle(u):
        own_copy(u).wait()
        each(1, cell, lambda k: out_copy(peer_of(k), peer_of(k), u).wait_recv())
        each(1, cell, lambda k: out_copy(peer_of(k), me, u).wait_send())
        each(1, teams, lambda k: each(0, near, lambda i: sum_copy(team_of(k), team, i, u).wait_send()))

    each(0, units, settle)
    each(1, cell, lambda k: ids_copy(peer_of(k), me).wait_send())
    each(1, cell, lambda k: each(0, units, lambda u: block_copy(peer_of(k), me, u, whole_slots).wait_send()))


def reduced_parts(jac, normals, counts, owner, where, crossing, tiles):
    slots, _, points, both = jac.shape
    orbits = crossing.shape[0]
    params = both // 2
    step = min(16, slots)
    groups = slots // step
    near = 2 if tiles % 2 == 0 and params * params % (2 * orbits * LANES) == 0 else 1
    cell, teams = near * orbits, tiles // near
    units = params * params // LANES // cell
    share = PAIR_ORB // tiles
    rank = orbits // 2 * share
    f32 = jnp.float32
    dma = pltpu.SemaphoreType.DMA
    return pl.pallas_call(
        reduce_kernel,
        in_specs=[pl.BlockSpec(memory_space=pl.ANY)] * 5 + [pl.BlockSpec(memory_space=pltpu.SMEM)],
        out_specs=pl.BlockSpec(memory_space=pl.ANY),
        out_shape=jax.ShapeDtypeStruct((cell, units, share, LANES), f32),
        scratch_shapes=[
            pltpu.VMEM(counts.shape, jnp.int32),
            pltpu.VMEM(owner.shape, jnp.int32),
            pltpu.VMEM(where.shape, jnp.int32),
            pltpu.VMEM(normals.shape, f32),
            pltpu.VMEM((slots, points), f32),
            pltpu.VMEM((slots, points), f32),
            pltpu.VMEM((8, slots), jnp.int32),
            pltpu.VMEM((orbits, 8, LANES), jnp.int32),
            pltpu.VMEM(jac.shape, jac.dtype),
            pltpu.VMEM((units, cell, slots, LANES), f32),
            pltpu.VMEM((units, cell, slots, LANES), f32),
            pltpu.VMEM((cell, 8, slots), jnp.int32),
            pltpu.VMEM((teams, near, rank, cell * slots), jnp.bfloat16),
            pltpu.VMEM((units, cell * slots, 2 * LANES), jnp.bfloat16),
            pltpu.VMEM((tiles, units, rank, LANES), f32),
            pltpu.VMEM((teams, near, units, rank, LANES), f32),
            pltpu.VMEM((cell, units, share, LANES), f32),
            pltpu.VMEM((step * params, params), f32),
            dma((3,)),
            pltpu.SemaphoreType.DMA,
            dma((groups,)),
            dma((cell,)),
            dma((cell,)),
            dma((units, cell)),
            dma((units, cell)),
            dma((teams, near, units)),
            dma((teams, near, units)),
            dma((cell, units)),
            dma((cell, units)),
            dma((units,)),
        ],
        compiler_params=pltpu.CompilerParams(
            collective_id=0, has_side_effects=True, vmem_limit_bytes=60 * 1024 * 1024
        ),
    )(jac, normals, counts, owner, where, crossing)


def assemble_kernel(crossing_ref, fin_ref, out_ref, turned):
    orbit = lax.axis_index("orbit")
    leads = crossing_ref[orbit] > orbit
    count, share, _ = fin_ref.shape
    params = 2 * count
    half = LANES // 2

    @pl.when(leads)
    def _():
        for m in range(count):
            first = (2 * m) % count
            side = (2 * m) // count * half
            out_ref[:, m * LANES : (m + 1) * LANES] = jnp.concatenate(
                [fin_ref[first + i, :, side : side + half] for i in range(2)], axis=1
            )

    @pl.when(jnp.logical_not(leads))
    def _():
        for unit in range(count):
            turned[unit * LANES : (unit + 1) * LANES, :] = jnp.transpose(fin_ref[unit])
        for m in range(count):
            rows = [turned[pl.ds(2 * m + k + h * params, count, stride=LANES), :] for k in range(2) for h in range(2)]
            out_ref[:, m * LANES : (m + 1) * LANES] = jnp.transpose(jnp.concatenate(rows, axis=0))


def assembled(crossing, fin):
    count, share, _ = fin.shape
    vmem = pl.BlockSpec(memory_space=pltpu.VMEM)
    return pl.pallas_call(
        assemble_kernel,
        in_specs=[pl.BlockSpec(memory_space=pltpu.SMEM), vmem],
        out_specs=vmem,
        out_shape=jax.ShapeDtypeStruct((share, count * LANES), jnp.float32),
        scratch_shapes=[pltpu.VMEM((count * LANES, share), jnp.float32)],
        compiler_params=pltpu.CompilerParams(vmem_limit_bytes=16 * 1024 * 1024),
    )(crossing, fin)


def local(jacobians, point_normals, block_counts, pair_owner, pair_local, crossing):
    tiles = lax.axis_size("tile")
    jac = jnp.transpose(jacobians, (0, 2, 1, 3))
    normals = jnp.transpose(point_normals, (1, 0, 2))
    owner, where = pair_owner.reshape(1, -1), pair_local.reshape(1, -1)
    fin = reduced_parts(jac, normals, block_counts, owner, where, crossing, tiles)
    return assembled(crossing, fin.reshape(-1, PAIR_ORB // tiles, LANES))[None]


def solution(mesh):
    in_specs = (
        P(("tile", "orbit"), None, None, None),
        P(("tile", "orbit"), None, None),
        P(("tile", "orbit"), None),
        P(("tile", "orbit"), None),
        P(("tile", "orbit")),
        P(),
    )
    out_specs = P("orbit", "tile", None)
    return jax.shard_map(local, mesh=mesh, in_specs=in_specs, out_specs=out_specs, check_vma=False)
```
